32 devices in a mesh: rows: 8 (over y, x, core), lags: 4 (over z).
Axes of the slice: x: 2, y: 2, z: 4, core: 2. Of those that a mesh axis runs over, the one named last changes fastest.
Arguments:
- history: float32 [32, 16, 2048], P('lags', None, 'rows'), may hold values from -6 to 6
- incident: float32 [2, 16, 2048], P(None, None, 'rows'), may hold values from -6 to 6
- kernel: float32 [8, 32, 6, 256, 256], P('rows', 'lags'), may hold values from -0.02734375 to 0.02734375
- near_blocks: int32 [8, 32, 6], P('rows', 'lags'), may hold values from 0 to 7, as said below
- self_inverse: float32 [8, 256, 256], P('rows'), may hold values from -1 to 1
Outputs:
- densities: float32 [2, 16, 2048], P(None, None, 'rows')
The draws below stay inside these ranges and needn't reach their ends.
Inputs may be any that keep to these rules, and one draw needn't show every extreme that they name: `near_blocks`: indices of source blocks; for each row block and each group of 8 consecutive lags, no source block appears more than 6 times among its 48 entries, and some block appears exactly 6 times.
All inputs are finite; a program needn't handle non-finite values.
Results may differ from the reference program's by a relative error of at most 0.00012.
Values sent between devices are 32-bit elements; how exact they have to be, the bound alone decides.
A program may use at most 128 MiB of HBM per device.

```python
import math
import jax
import jax.numpy as jnp
from jax import lax

BLOCK = 256
W = 16
LAG_DEV = 8
NEAR = 6
STEPS = 2
LAGS = 32
NB = 8
N = 2048
MOST = 6


def draw_self_inverse(key, part):
    spread = 0.3 / math.sqrt(BLOCK)
    noise = spread * jax.random.truncated_normal(key, -4.0, 4.0, (NB, BLOCK, BLOCK), jnp.float32)
    return noise + 0.5 * jnp.eye(BLOCK, dtype=jnp.float32)[None]


def draw_near_blocks(key, part):
    groups = LAGS // LAG_DEV
    slot_total = LAG_DEV * NEAR
    base = jax.random.fold_in(key, 7)

    def one_group(group_key):
        first_key, second_key = jax.random.split(group_key)
        perm_keys = jax.random.split(first_key, MOST)
        perms = jax.vmap(lambda inner: jax.random.permutation(inner, NB))(perm_keys)
        listed = perms.reshape(MOST * NB)[:slot_total].astype(jnp.int32)
        return jax.random.permutation(second_key, listed)
    group_keys = jax.random.split(base, NB * groups)
    drawn = jax.vmap(one_group)(group_keys)
    return drawn.reshape(NB, groups * LAG_DEV, NEAR).astype(jnp.int32)


def levels(rng, extent, cuts, smallest, top_value):
    def one(position, parts):
        heights = jax.random.uniform(jax.random.fold_in(jax.random.fold_in(rng, 6), position), (parts,), jnp.float32, smallest / len(cuts), top_value / len(cuts))
        return jnp.repeat(jnp.exp(heights), extent[position] // parts).reshape((-1,) + (1,) * (len(extent) - position - 1))

    level = one(*cuts[0])
    for cut in cuts[1:]:
        level = level * one(*cut)
    return level


def bell_draw(own_key, shape, scale, most, cuts=(), kind=jnp.bfloat16):
    entries = jax.random.normal(own_key, shape, jnp.float32) * scale
    if len(cuts) > 0:
        entries = levels(own_key, shape, cuts, -0.22, 0.18) * entries
    return jnp.clip(entries, min=-most, max=most).astype(kind)


def setup_inputs(seed: int = 0) -> dict:
    key_of = jax.random.split(jax.random.key(seed), 6)
    return {
        "history": bell_draw(key_of[0], (LAGS, W, N), 0.7, 6.0, ((0, 4), (2, 8)), jnp.float32),
        "incident": bell_draw(key_of[1], (STEPS, W, N), 1.0, 6.0, ((2, 8),), jnp.float32),
        "kernel": bell_draw(key_of[2], (NB, LAGS, NEAR, BLOCK, BLOCK), (NEAR * LAGS * BLOCK) ** -0.5, 0.02734375, ((0, 8), (1, 4)), jnp.float32),
        "near_blocks": draw_near_blocks(jax.random.fold_in(key_of[5], 71), 0),
        "self_inverse": draw_self_inverse(jax.random.fold_in(key_of[5], 71), 0),
    }


def reference(history, incident, kernel, near_blocks, self_inverse):
    highest = lax.Precision.HIGHEST
    past_window = history.reshape(LAGS, W, NB, BLOCK)
    outputs = []
    for instant in range(STEPS):
        def one_block(operands):
            kernel_rows, source_ids = operands
            lag_index = jnp.arange(LAGS, dtype=jnp.int32)[:, None]
            picked = past_window[lag_index, :, source_ids]
            return jnp.einsum("lkwc,lkcr->wr", picked, kernel_rows, precision=highest)

        fields = lax.map(one_block, (kernel, near_blocks))
        near_field = jnp.transpose(fields, (1, 0, 2))
        driven = incident[instant].reshape(W, NB, BLOCK) - near_field
        density = jnp.einsum("wic,icr->wir", driven, self_inverse, precision=highest)
        outputs.append(density.reshape(W, NB * BLOCK))
        past_window = jnp.concatenate([density[None], past_window[:-1]], axis=0)
    return jnp.stack(outputs)
```

```python
import functools

import jax
import jax.numpy as jnp
from jax import lax
from jax.experimental import pallas as pl
from jax.experimental.pallas import tpu as pltpu
from jax.sharding import PartitionSpec as P

MESH = pl.DeviceIdType.MESH
VMEM_LIMIT = 58 * 1024 * 1024


def split(x):
    high = x.astype(jnp.bfloat16)
    low = (x - high.astype(jnp.float32)).astype(jnp.bfloat16)
    return high, low


def product(x, high, low):
    m = x.shape[0]
    xh, xl = split(x)
    both = jnp.dot(jnp.concatenate([xh, xl], 0), high, preferred_element_type=jnp.float32)
    rest = jnp.dot(xh, low, preferred_element_type=jnp.float32)
    return both[:m] + (both[m:] + rest)


def march(
    rows, groups, per_chunk,
    near, hist, inc_hbm, ker, inv_hbm, out,
    kbuf, khigh, klow, extra, acc, part, dens, inc, inv, ihigh, ilow,
    ker_sem, in_sem, own_sem, out_sem,
    send_sem, direct_sem, pass_send, pass_sem,
    extra_send, extra_sem, epass_send, epass_sem,
    part_send, part_sem, dens_send, dens_sem, res_send, res_sem,
    *past,
):
    lags, waves, block = hist.shape
    steps = inc_hbm.shape[0]
    slots = near.shape[0]
    ahead = steps - 1
    half = rows // 2
    chunks = lags // per_chunk
    row = lax.axis_index("rows")
    group = lax.axis_index("lags")
    core = lax.rem(row, 2)
    place = lax.div(row, 2)
    partner = row + 1 - 2 * core

    def remote(src, dst, send, recv, r, g):
        return pltpu.make_async_remote_copy(
            src_ref=src, dst_ref=dst, send_sem=send, recv_sem=recv,
            device_id=(r, g), device_id_type=MESH,
        )

    def all_of(ref, sem):
        pltpu.make_async_copy(ref, ref, sem).wait()

    def lags_of(c):
        return hist.at[pl.ds(c * per_chunk, per_chunk)]

    own = [
        pltpu.make_async_copy(lags_of(c), past[c].at[core, place], own_sem.at[c])
        for c in range(chunks)
    ]
    for copy in own:
        copy.start()
    loads = [pltpu.make_async_copy(ker.at[0, j], kbuf.at[j], ker_sem.at[j]) for j in range(lags)]
    inc_load = pltpu.make_async_copy(inc_hbm, inc, in_sem.at[0])
    inv_load = pltpu.make_async_copy(inv_hbm.at[0], inv, in_sem.at[1])

    barrier = pltpu.get_barrier_semaphore()

    def greet(r, g):
        pl.semaphore_signal(barrier, inc=1, device_id=(r, g), device_id_type=MESH)

    for m in range(1, rows):
        greet(lax.rem(row + m, rows), group)
    for m in range(1, groups):
        greet(row, lax.rem(group + m, groups))

    @pl.when(group > 0)
    def _():
        for m in range(1, half):
            greet(lax.rem(row + 2 * m, rows), group - 1)

    @pl.when(group < groups - 1)
    def _():
        for m in range(1, half):
            greet(lax.rem(row + 2 * m, rows), group + 1)

    for load in loads:
        load.start()
    inv_load.start()
    inc_load.start()

    sides = (group > 0).astype(jnp.int32) + (group < groups - 1).astype(jnp.int32)
    pl.semaphore_wait(barrier, rows - 1 + groups - 1 + (half - 1) * sides)

    def chunk_copy(c, m):
        return remote(
            lags_of(c), past[c].at[core, place],
            send_sem.at[c], direct_sem.at[c], lax.rem(row + 2 * m, rows), group,
        )

    def chunk_pass(c):
        ref = past[c].at[core]
        return remote(ref, ref, pass_send.at[c], pass_sem.at[c], partner, group)

    def extra_copy(m, g):
        return remote(
            hist.at[pl.ds(lags - ahead, ahead)], extra.at[core, place],
            extra_send, extra_sem, lax.rem(row + 2 * m, rows), g,
        )

    def extra_pass():
        ref = extra.at[core]
        return remote(ref, ref, epass_send, epass_sem, partner, group)

    for c in range(chunks):
        for m in range(1, half):
            chunk_copy(c, m).start()
        if c == 0 and ahead > 0:

            @pl.when(group < groups - 1)
            def _():
                for m in range(half):
                    extra_copy(m, group + 1).start()

    if ahead > 0:

        @pl.when(group == 0)
        def _():
            extra[...] = jnp.zeros(extra.shape, jnp.float32)

    def convert(j):
        loads[j].wait()

        @pl.loop(0, slots)
        def _(k):
            high, low = split(kbuf[j, k])
            at = pl.ds(pl.multiple_of(k * block, block), block)
            khigh[j, at] = high
            klow[j, at] = low

    def pass_on(c):
        own[c].wait()
        if half > 1:
            all_of(past[c].at[core, pl.ds(0, half - 1)], direct_sem.at[c])
        chunk_pass(c).start()

    def entry(h, b):
        at = (lax.rem(b, 2), lax.div(b, 2))
        if h < 0:
            return extra[at[0], at[1], h + ahead]
        return past[h // per_chunk][at[0], at[1], h % per_chunk]

    def multiply(c):
        chunk_pass(c).wait_recv()
        for j in range(c * per_chunk, (c + 1) * per_chunk):
            pieces = []
            for k in range(slots):
                b = near[k, 0, j]
                pieces.append(jnp.concatenate([entry(j - s, b) for s in range(ahead, -1, -1)], 0))
            value = product(jnp.concatenate(pieces, 1), khigh[j], klow[j])
            value = value.reshape(steps, waves, block)
            if j == 0:
                acc[...] = value
            else:
                acc[...] += value

    done = 0
    for c in range(chunks):
        for j in range(c * per_chunk, (c + 1) * per_chunk):
            convert(j)
        pass_on(c)
        if c == min(1, chunks - 1) and ahead > 0:

            @pl.when(group > 0)
            def _():
                all_of(extra.at[core], extra_sem)
                extra_pass().start()

        if c >= 2:
            if done == 0 and ahead > 0:

                @pl.when(group > 0)
                def _():
                    extra_pass().wait_recv()

            multiply(done)
            done += 1
    if done == 0 and ahead > 0:

        @pl.when(group > 0)
        def _():
            extra_pass().wait_recv()

    inv_load.wait()
    ihigh[...], ilow[...] = split(inv[...])
    for c in range(done, chunks):
        multiply(c)

    def part_copy(s, to):
        t = ahead - s
        return remote(acc.at[t], part.at[group, t], part_send.at[s], part_sem.at[s], row, to)

    def result_copy(s, g):
        return remote(dens.at[s, row], out.at[s], res_send.at[s], res_sem.at[s], row, g)

    def dens_copy(s, m):
        ref = dens.at[s, row]
        return remote(ref, ref, dens_send.at[s], dens_sem.at[s], lax.rem(row + m, rows), group)

    inc_load.wait()

    @pl.when(group > 0)
    def _():
        for s in range(steps):
            part_copy(s, 0).start()
        for s in range(steps):
            part_copy(s, 0).wait_send()
        for s in range(steps):
            result_copy(s, 0).wait_recv()

    @pl.when(group == 0)
    def _():
        def keep(s):
            return pltpu.make_async_copy(dens.at[s, row], out.at[s], out_sem.at[s])

        for s in range(steps):
            t = ahead - s
            all_of(part.at[pl.ds(0, groups - 1), t], part_sem.at[s])
            near_field = acc[t]
            for g in range(1, groups):
                near_field = near_field + part[g, t]
            if s > 0:
                all_of(dens.at[s - 1, pl.ds(0, rows - 1)], dens_sem.at[s - 1])
            for q in range(s):
                j = s - 1 - q
                picked = jnp.concatenate([dens[q, near[k, 0, j]] for k in range(slots)], 1)
                near_field = near_field + product(picked, khigh[j], klow[j])
            dens[s, row] = product(inc[s] - near_field, ihigh[...], ilow[...])
            if s < steps - 1:
                for m in range(1, rows):
                    dens_copy(s, m).start()
            for g in range(1, groups):
                result_copy(s, g).start()
            keep(s).start()
        for s in range(steps):
            if s < steps - 1:
                all_of(dens.at[s, pl.ds(0, rows - 1)], dens_send.at[s])
            all_of(dens.at[s, pl.ds(0, groups - 1)], res_send.at[s])
            keep(s).wait()

    for c in range(chunks):
        if half > 1:
            all_of(past[c].at[core, pl.ds(0, half - 1)], send_sem.at[c])
        chunk_pass(c).wait_send()
    if ahead > 0:

        @pl.when(group < groups - 1)
        def _():
            all_of(extra.at[core], extra_send)

        @pl.when(group > 0)
        def _():
            extra_pass().wait_send()


def solution(mesh):
    rows, groups = mesh.shape["rows"], mesh.shape["lags"]

    def shards(history, incident, kernel, near_blocks, self_inverse):
        lags, waves, block = history.shape
        steps = incident.shape[0]
        slots = near_blocks.shape[2]
        per_chunk = 2 if lags % 2 == 0 else 1
        chunks = lags // per_chunk
        half = rows // 2
        ahead = steps - 1
        f32, bf16 = jnp.float32, jnp.bfloat16
        dma = pltpu.SemaphoreType.DMA
        anywhere = pl.BlockSpec(memory_space=pl.ANY)
        return pl.pallas_call(
            functools.partial(march, rows, groups, per_chunk),
            out_shape=jax.ShapeDtypeStruct((steps, waves, block), f32),
            in_specs=[pl.BlockSpec(memory_space=pltpu.SMEM)] + [anywhere] * 4,
            out_specs=anywhere,
            scratch_shapes=[
                pltpu.VMEM((lags, slots, block, block), f32),
                pltpu.VMEM((lags, slots * block, block), bf16),
                pltpu.VMEM((lags, slots * block, block), bf16),
                pltpu.VMEM((2, half, max(ahead, 1), waves, block), f32),
                pltpu.VMEM((steps, waves, block), f32),
                pltpu.VMEM((groups, steps, waves, block), f32),
                pltpu.VMEM((steps, rows, waves, block), f32),
                pltpu.VMEM((steps, waves, block), f32),
                pltpu.VMEM((block, block), f32),
                pltpu.VMEM((block, block), bf16),
                pltpu.VMEM((block, block), bf16),
                dma((lags,)), dma((2,)), dma((chunks,)), dma((steps,)),
                dma((chunks,)), dma((chunks,)), dma((chunks,)), dma((chunks,)),
                dma, dma, dma, dma,
                dma((steps,)), dma((steps,)), dma((steps,)), dma((steps,)), dma((steps,)), dma((steps,)),
            ]
            + [pltpu.VMEM((2, half, per_chunk, waves, block), f32)] * chunks,
            compiler_params=pltpu.CompilerParams(
                collective_id=0, has_side_effects=True, vmem_limit_bytes=VMEM_LIMIT
            ),
            cost_estimate=pl.CostEstimate(
                flops=6 * steps * lags * slots * waves * block * block,
                bytes_accessed=4 * lags * slots * block * block,
                transcendentals=0,
            ),
        )(jnp.transpose(near_blocks, (2, 0, 1)), history, incident, kernel, self_inverse)

    in_specs = (
        P("lags", None, "rows"),
        P(None, None, "rows"),
        P("rows", "lags", None, None, None),
        P("rows", "lags", None),
        P("rows", None, None),
    )
    return jax.shard_map(
        shards, mesh=mesh, in_specs=in_specs, out_specs=P(None, None, "rows"), check_vma=False
    )
```

```python
import functools

import jax
import jax.numpy as jnp
from jax import lax
from jax.experimental import pallas as pl
from jax.experimental.pallas import tpu as pltpu
from jax.sharding import PartitionSpec as P

MESH = pl.DeviceIdType.MESH
VMEM_LIMIT = 58 * 1024 * 1024


def split(x):
    high = x.astype(jnp.bfloat16)
    low = (x - high.astype(jnp.float32)).astype(jnp.bfloat16)
    return high, low


def product(x, high, low):
    m = x.shape[0]
    xh, xl = split(x)
    both = jnp.dot(jnp.concatenate([xh, xl], 0), high, preferred_element_type=jnp.float32)
    rest = jnp.dot(xh, low, preferred_element_type=jnp.float32)
    return both[:m] + (both[m:] + rest)


def march(
    rows, groups, per_chunk,
    near, hist, inc_hbm, ker, inv_hbm, out,
    kbuf, khigh, klow, extra, acc, part, dens, inc, inv, ihigh, ilow,
    ker_sem, in_sem, own_sem, out_sem,
    send_sem, direct_sem, pass_send, pass_sem,
    extra_send, extra_sem, epass_send, epass_sem,
    relay_send, relay_sem, part_send, part_sem, dens_send, dens_sem, res_send, res_sem,
    *past,
):
    lags, waves, block = hist.shape
    steps = inc_hbm.shape[0]
    slots = near.shape[0]
    ahead = steps - 1
    half = rows // 2
    chunks = lags // per_chunk
    row = lax.axis_index("rows")
    group = lax.axis_index("lags")
    core = lax.rem(row, 2)
    place = lax.div(row, 2)
    partner = row + 1 - 2 * core
    square = rows == 8

    def remote(src, dst, send, recv, r, g):
        return pltpu.make_async_remote_copy(
            src_ref=src, dst_ref=dst, send_sem=send, recv_sem=recv,
            device_id=(r, g), device_id_type=MESH,
        )

    def all_of(ref, sem):
        pltpu.make_async_copy(ref, ref, sem).wait()

    def lags_of(c):
        return hist.at[pl.ds(c * per_chunk, per_chunk)]

    own = [
        pltpu.make_async_copy(lags_of(c), past[c].at[core, place], own_sem.at[c])
        for c in range(chunks)
    ]
    for copy in own:
        copy.start()
    loads = [pltpu.make_async_copy(ker.at[0, j], kbuf.at[j], ker_sem.at[j]) for j in range(lags)]
    inc_load = pltpu.make_async_copy(inc_hbm, inc, in_sem.at[0])
    inv_load = pltpu.make_async_copy(inv_hbm.at[0], inv, in_sem.at[1])

    barrier = pltpu.get_barrier_semaphore()

    def peer(m):
        return jnp.bitwise_xor(row, m) if square else lax.rem(row + m, rows)

    def greet(r, g):
        pl.semaphore_signal(barrier, inc=1, device_id=(r, g), device_id_type=MESH)

    for m in range(1, groups):
        greet(row, lax.rem(group + m, groups))

    @pl.when(group > 0)
    def _():
        for m in range(1, half):
            greet(lax.rem(row + 2 * m, rows), group - 1)

    @pl.when(group < groups - 1)
    def _():
        for m in range(1, half):
            greet(lax.rem(row + 2 * m, rows), group + 1)

    for m in range(rows - 1, 0, -1):
        greet(peer(m), group)

    for load in loads:
        load.start()
    inv_load.start()
    inc_load.start()

    def convert(j):
        loads[j].wait()

        @pl.loop(0, slots)
        def _(k):
            high, low = split(kbuf[j, k])
            at = pl.ds(pl.multiple_of(k * block, block), block)
            khigh[j, at] = high
            klow[j, at] = low

    early = min(0, lags)
    for j in range(early):
        convert(j)

    sides = (group > 0).astype(jnp.int32) + (group < groups - 1).astype(jnp.int32)
    pl.semaphore_wait(barrier, rows - 1 + groups - 1 + (half - 1) * sides)

    def chunk_copy(c, m):
        return remote(
            lags_of(c), past[c].at[core, place],
            send_sem.at[c], direct_sem.at[c], peer(2 * m), group,
        )

    relayed = [False for c in range(chunks)]

    def chunk_relay(c):
        first, second = (4, 2) if c % 2 == 0 else (2, 4)
        ref = past[c].at[core, lax.div(jnp.bitwise_xor(row, first), 2)]
        return remote(
            ref, ref, relay_send.at[c], relay_sem.at[c], jnp.bitwise_xor(row, second), group
        )

    def straight(c):
        return range(1, half - 1) if relayed[c] else range(half - 1, 0, -1)

    def chunk_pass(c):
        ref = past[c].at[core]
        return remote(ref, ref, pass_send.at[c], pass_sem.at[c], partner, group)

    def extra_copy(m, g):
        return remote(
            hist.at[pl.ds(lags - ahead, ahead)], extra.at[core, place],
            extra_send, extra_sem, lax.rem(row + 2 * m, rows), g,
        )

    def extra_pass():
        ref = extra.at[core]
        return remote(ref, ref, epass_send, epass_sem, partner, group)

    for c in range(chunks):
        for m in straight(c):
            chunk_copy(c, m).start()
        if c == 0 and ahead > 0:

            @pl.when(group < groups - 1)
            def _():
                for m in range(half):
                    extra_copy(m, group + 1).start()

    if ahead > 0:

        @pl.when(group == 0)
        def _():
            extra[...] = jnp.zeros(extra.shape, jnp.float32)

    def relay(c):
        own[c].wait()
        if half > 1:
            all_of(past[c].at[core, pl.ds(0, len(straight(c)))], direct_sem.at[c])
        if relayed[c]:
            chunk_relay(c).start()

    def pass_on(c):
        if relayed[c]:
            chunk_relay(c).wait_recv()
        chunk_pass(c).start()

    def entry(h, b):
        at = (lax.rem(b, 2), lax.div(b, 2))
        if h < 0:
            return extra[at[0], at[1], h + ahead]
        return past[h // per_chunk][at[0], at[1], h % per_chunk]

    def multiply(c):
        chunk_pass(c).wait_recv()
        for j in range(c * per_chunk, (c + 1) * per_chunk):
            pieces = []
            for k in range(slots):
                b = near[k, 0, j]
                pieces.append(jnp.concatenate([entry(j - s, b) for s in range(ahead, -1, -1)], 0))
            value = product(jnp.concatenate(pieces, 1), khigh[j], klow[j])
            value = value.reshape(steps, waves, block)
            if j == 0:
                acc[...] = value
            else:
                acc[...] += value

    def extra_in():
        if ahead > 0:

            @pl.when(group > 0)
            def _():
                all_of(extra.at[core], extra_sem)
                extra_pass().start()

    def extra_wait():
        if ahead > 0:

            @pl.when(group > 0)
            def _():
                extra_pass().wait_recv()

    turn = early
    inv_at = max(chunks - 2, 0)
    for c in range(chunks):
        upto = min(lags, max(turn, 0 + (c + 1) * per_chunk))
        for j in range(turn, upto):
            convert(j)
        turn = upto
        relay(c)
        if not relayed[c]:
            pass_on(c)
        if c >= 1 and relayed[c - 1]:
            pass_on(c - 1)
        if c == chunks // 2 - 1:
            extra_in()
        if c == inv_at:
            inv_load.wait()
            ihigh[...], ilow[...] = split(inv[...])
        if c >= 2:
            if c == 2:
                extra_wait()
            multiply(c - 2)
    for c in range(max(chunks - 2, 0), chunks):
        multiply(c)

    def part_copy(s, to):
        t = ahead - s
        return remote(acc.at[t], part.at[group, t], part_send.at[s], part_sem.at[s], row, to)

    def result_copy(s, g):
        return remote(dens.at[s, row], out.at[s], res_send.at[s], res_sem.at[s], row, g)

    def dens_copy(s, m):
        ref = dens.at[s, row]
        return remote(ref, ref, dens_send.at[s], dens_sem.at[s], peer(m), group)

    inc_load.wait()

    @pl.when(group > 0)
    def _():
        for s in range(steps):
            part_copy(s, 0).start()
        for s in range(steps):
            part_copy(s, 0).wait_send()
        for s in range(steps):
            result_copy(s, 0).wait_recv()

    @pl.when(group == 0)
    def _():
        def keep(s):
            return pltpu.make_async_copy(dens.at[s, row], out.at[s], out_sem.at[s])

        for s in range(steps):
            t = ahead - s
            all_of(part.at[pl.ds(0, groups - 1), t], part_sem.at[s])
            near_field = acc[t]
            for g in range(1, groups):
                near_field = near_field + part[g, t]
            if s > 0:
                all_of(dens.at[s - 1, pl.ds(0, rows - 1)], dens_sem.at[s - 1])
            for q in range(s):
                j = s - 1 - q
                picked = jnp.concatenate([dens[q, near[k, 0, j]] for k in range(slots)], 1)
                near_field = near_field + product(picked, khigh[j], klow[j])
            dens[s, row] = product(inc[s] - near_field, ihigh[...], ilow[...])
            if s < steps - 1:
                for m in range(rows - 1, 0, -1):
                    dens_copy(s, m).start()
            for g in range(1, groups):
                result_copy(s, g).start()
            keep(s).start()
        for s in range(steps):
            if s < steps - 1:
                all_of(dens.at[s, pl.ds(0, rows - 1)], dens_send.at[s])
            all_of(dens.at[s, pl.ds(0, groups - 1)], res_send.at[s])
            keep(s).wait()

    for c in range(chunks):
        if half > 1:
            all_of(past[c].at[core, pl.ds(0, len(straight(c)))], send_sem.at[c])
        if relayed[c]:
            chunk_relay(c).wait_send()
        chunk_pass(c).wait_send()
    if ahead > 0:

        @pl.when(group < groups - 1)
        def _():
            all_of(extra.at[core], extra_send)

        @pl.when(group > 0)
        def _():
            extra_pass().wait_send()


def solution(mesh):
    rows, groups = mesh.shape["rows"], mesh.shape["lags"]

    def shards(history, incident, kernel, near_blocks, self_inverse):
        lags, waves, block = history.shape
        steps = incident.shape[0]
        slots = near_blocks.shape[2]
        per_chunk = 2 if lags % 2 == 0 else 1
        chunks = lags // per_chunk
        half = rows // 2
        ahead = steps - 1
        f32, bf16 = jnp.float32, jnp.bfloat16
        dma = pltpu.SemaphoreType.DMA
        anywhere = pl.BlockSpec(memory_space=pl.ANY)
        return pl.pallas_call(
            functools.partial(march, rows, groups, per_chunk),
            out_shape=jax.ShapeDtypeStruct((steps, waves, block), f32),
            in_specs=[pl.BlockSpec(memory_space=pltpu.SMEM)] + [anywhere] * 4,
            out_specs=anywhere,
            scratch_shapes=[
                pltpu.VMEM((lags, slots, block, block), f32),
                pltpu.VMEM((lags, slots * block, block), bf16),
                pltpu.VMEM((lags, slots * block, block), bf16),
                pltpu.VMEM((2, half, max(ahead, 1), waves, block), f32),
                pltpu.VMEM((steps, waves, block), f32),
                pltpu.VMEM((groups, steps, waves, block), f32),
                pltpu.VMEM((steps, rows, waves, block), f32),
                pltpu.VMEM((steps, waves, block), f32),
                pltpu.VMEM((block, block), f32),
                pltpu.VMEM((block, block), bf16),
                pltpu.VMEM((block, block), bf16),
                dma((lags,)), dma((2,)), dma((chunks,)), dma((steps,)),
                dma((chunks,)), dma((chunks,)), dma((chunks,)), dma((chunks,)),
                dma, dma, dma, dma, dma((chunks,)), dma((chunks,)),
                dma((steps,)), dma((steps,)), dma((steps,)), dma((steps,)), dma((steps,)), dma((steps,)),
            ]
            + [pltpu.VMEM((2, half, per_chunk, waves, block), f32)] * chunks,
            compiler_params=pltpu.CompilerParams(
                collective_id=0, has_side_effects=True, vmem_limit_bytes=VMEM_LIMIT
            ),
            cost_estimate=pl.CostEstimate(
                flops=6 * steps * lags * slots * waves * block * block,
                bytes_accessed=4 * lags * slots * block * block,
                transcendentals=0,
            ),
        )(jnp.transpose(near_blocks, (2, 0, 1)), history, incident, kernel, self_inverse)

    in_specs = (
        P("lags", None, "rows"),
        P(None, None, "rows"),
        P("rows", "lags", None, None, None),
        P("rows", "lags", None),
        P("rows", None, None),
    )
    return jax.shard_map(
        shards, mesh=mesh, in_specs=in_specs, out_specs=P(None, None, "rows"), check_vma=False
    )
```

```python
import functools

import jax
import jax.numpy as jnp
from jax import lax
from jax.experimental import pallas as pl
from jax.experimental.pallas import tpu as pltpu
from jax.sharding import PartitionSpec as P

MESH = pl.DeviceIdType.MESH
VMEM_LIMIT = 58 * 1024 * 1024


def split(x):
    high = x.astype(jnp.bfloat16)
    low = (x - high.astype(jnp.float32)).astype(jnp.bfloat16)
    return high, low


def product(x, high, low):
    m = x.shape[0]
    xh, xl = split(x)
    both = jnp.dot(jnp.concatenate([xh, xl], 0), high, preferred_element_type=jnp.float32)
    rest = jnp.dot(xh, low, preferred_element_type=jnp.float32)
    return both[:m] + (both[m:] + rest)


def march(
    rows, groups, per_chunk,
    near, hist, inc_hbm, ker, inv_hbm, out,
    kbuf, khigh, klow, extra, acc, part, dens, inc, inv, ihigh, ilow,
    ker_sem, in_sem, own_sem, out_sem,
    send_sem, direct_sem, pass_send, pass_sem,
    extra_send, extra_sem, epass_send, epass_sem,
    relay_send, relay_sem, part_send, part_sem, dens_send, dens_sem, res_send, res_sem,
    *past,
):
    lags, waves, block = hist.shape
    steps = inc_hbm.shape[0]
    slots = near.shape[0]
    ahead = steps - 1
    half = rows // 2
    chunks = lags // per_chunk
    row = lax.axis_index("rows")
    group = lax.axis_index("lags")
    core = lax.rem(row, 2)
    place = lax.div(row, 2)
    partner = row + 1 - 2 * core
    square = rows == 8

    def remote(src, dst, send, recv, r, g):
        return pltpu.make_async_remote_copy(
            src_ref=src, dst_ref=dst, send_sem=send, recv_sem=recv,
            device_id=(r, g), device_id_type=MESH,
        )

    def all_of(ref, sem):
        pltpu.make_async_copy(ref, ref, sem).wait()

    def lags_of(c):
        return hist.at[pl.ds(c * per_chunk, per_chunk)]

    own = [
        pltpu.make_async_copy(lags_of(c), past[c].at[core, place], own_sem.at[c])
        for c in range(chunks)
    ]
    for copy in own:
        copy.start()
    loads = [pltpu.make_async_copy(ker.at[0, j], kbuf.at[j], ker_sem.at[j]) for j in range(lags)]
    inc_load = pltpu.make_async_copy(inc_hbm, inc, in_sem.at[0])
    inv_load = pltpu.make_async_copy(inv_hbm.at[0], inv, in_sem.at[1])

    barrier = pltpu.get_barrier_semaphore()

    def peer(m):
        return jnp.bitwise_xor(row, m) if square else lax.rem(row + m, rows)

    def greet(r, g):
        pl.semaphore_signal(barrier, inc=1, device_id=(r, g), device_id_type=MESH)

    for m in range(1, groups):
        greet(row, lax.rem(group + m, groups))

    @pl.when(group > 0)
    def _():
        for m in range(1, half):
            greet(lax.rem(row + 2 * m, rows), group - 1)

    @pl.when(group < groups - 1)
    def _():
        for m in range(1, half):
            greet(lax.rem(row + 2 * m, rows), group + 1)

    for m in range(rows - 1, 0, -1):
        greet(peer(m), group)

    for load in loads:
        load.start()
    inv_load.start()
    inc_load.start()

    def convert(j):
        loads[j].wait()

        @pl.loop(0, slots)
        def _(k):
            high, low = split(kbuf[j, k])
            at = pl.ds(pl.multiple_of(k * block, block), block)
            khigh[j, at] = high
            klow[j, at] = low

    early = min(0, lags)
    for j in range(early):
        convert(j)

    for copy in own:
        copy.wait()

    sides = (group > 0).astype(jnp.int32) + (group < groups - 1).astype(jnp.int32)
    pl.semaphore_wait(barrier, rows - 1 + groups - 1 + (half - 1) * sides)

    def chunk_copy(c, m):
        return remote(
            past[c].at[core, place], past[c].at[core, place],
            send_sem.at[c], direct_sem.at[c], peer(2 * m), group,
        )

    relayed = [False for c in range(chunks)]

    def chunk_relay(c):
        first, second = (4, 2) if c % 2 == 0 else (2, 4)
        ref = past[c].at[core, lax.div(jnp.bitwise_xor(row, first), 2)]
        return remote(
            ref, ref, relay_send.at[c], relay_sem.at[c], jnp.bitwise_xor(row, second), group
        )

    def straight(c):
        return range(1, half - 1) if relayed[c] else range(half - 1, 0, -1)

    def chunk_pass(c):
        ref = past[c].at[core]
        return remote(ref, ref, pass_send.at[c], pass_sem.at[c], partner, group)

    def extra_copy(m, g):
        return remote(
            hist.at[pl.ds(lags - ahead, ahead)], extra.at[core, place],
            extra_send, extra_sem, lax.rem(row + 2 * m, rows), g,
        )

    def extra_pass():
        ref = extra.at[core]
        return remote(ref, ref, epass_send, epass_sem, partner, group)

    for c in range(chunks):
        for m in straight(c):
            chunk_copy(c, m).start()
        if c == 0 and ahead > 0:

            @pl.when(group < groups - 1)
            def _():
                for m in range(half):
                    extra_copy(m, group + 1).start()

    if ahead > 0:

        @pl.when(group == 0)
        def _():
            extra[...] = jnp.zeros(extra.shape, jnp.float32)

    def relay(c):
        if half > 1:
            all_of(past[c].at[core, pl.ds(0, len(straight(c)))], direct_sem.at[c])
        if relayed[c]:
            chunk_relay(c).start()

    def pass_on(c):
        if relayed[c]:
            chunk_relay(c).wait_recv()
        chunk_pass(c).start()

    def entry(h, b):
        at = (lax.rem(b, 2), lax.div(b, 2))
        if h < 0:
            return extra[at[0], at[1], h + ahead]
        return past[h // per_chunk][at[0], at[1], h % per_chunk]

    def multiply(c):
        chunk_pass(c).wait_recv()
        for j in range(c * per_chunk, (c + 1) * per_chunk):
            pieces = []
            for k in range(slots):
                b = near[k, 0, j]
                pieces.append(jnp.concatenate([entry(j - s, b) for s in range(ahead, -1, -1)], 0))
            value = product(jnp.concatenate(pieces, 1), khigh[j], klow[j])
            value = value.reshape(steps, waves, block)
            if j == 0:
                acc[...] = value
            else:
                acc[...] += value

    def extra_in():
        if ahead > 0:

            @pl.when(group > 0)
            def _():
                all_of(extra.at[core], extra_sem)
                extra_pass().start()

    def extra_wait():
        if ahead > 0:

            @pl.when(group > 0)
            def _():
                extra_pass().wait_recv()

    turn = early
    inv_at = max(chunks - 2, 0)
    for c in range(chunks):
        upto = min(lags, max(turn, 0 + (c + 1) * per_chunk))
        for j in range(turn, upto):
            convert(j)
        turn = upto
        relay(c)
        if not relayed[c]:
            pass_on(c)
        if c >= 1 and relayed[c - 1]:
            pass_on(c - 1)
        if c == chunks // 2 - 1:
            extra_in()
        if c == inv_at:
            inv_load.wait()
            ihigh[...], ilow[...] = split(inv[...])
        if c >= 2:
            if c == 2:
                extra_wait()
            multiply(c - 2)
    for c in range(max(chunks - 2, 0), chunks):
        multiply(c)

    def part_copy(s, to):
        t = ahead - s
        return remote(acc.at[t], part.at[group, t], part_send.at[s], part_sem.at[s], row, to)

    def result_copy(s, g):
        return remote(dens.at[s, row], out.at[s], res_send.at[s], res_sem.at[s], row, g)

    def dens_copy(s, m):
        ref = dens.at[s, row]
        return remote(ref, ref, dens_send.at[s], dens_sem.at[s], peer(m), group)

    inc_load.wait()

    @pl.when(group > 0)
    def _():
        for s in range(steps):
            part_copy(s, 0).start()
        for s in range(steps):
            part_copy(s, 0).wait_send()
        for s in range(steps):
            result_copy(s, 0).wait_recv()

    @pl.when(group == 0)
    def _():
        def keep(s):
            return pltpu.make_async_copy(dens.at[s, row], out.at[s], out_sem.at[s])

        for s in range(steps):
            t = ahead - s
            all_of(part.at[pl.ds(0, groups - 1), t], part_sem.at[s])
            near_field = acc[t]
            for g in range(1, groups):
                near_field = near_field + part[g, t]
            if s > 0:
                all_of(dens.at[s - 1, pl.ds(0, rows - 1)], dens_sem.at[s - 1])
            for q in range(s):
                j = s - 1 - q
                picked = jnp.concatenate([dens[q, near[k, 0, j]] for k in range(slots)], 1)
                near_field = near_field + product(picked, khigh[j], klow[j])
            dens[s, row] = product(inc[s] - near_field, ihigh[...], ilow[...])
            if s < steps - 1:
                for m in range(rows - 1, 0, -1):
                    dens_copy(s, m).start()
            for g in range(1, groups):
                result_copy(s, g).start()
            keep(s).start()
        for s in range(steps):
            if s < steps - 1:
                all_of(dens.at[s, pl.ds(0, rows - 1)], dens_send.at[s])
            all_of(dens.at[s, pl.ds(0, groups - 1)], res_send.at[s])
            keep(s).wait()

    for c in range(chunks):
        if half > 1:
            all_of(past[c].at[core, pl.ds(0, len(straight(c)))], send_sem.at[c])
        if relayed[c]:
            chunk_relay(c).wait_send()
        chunk_pass(c).wait_send()
    if ahead > 0:

        @pl.when(group < groups - 1)
        def _():
            all_of(extra.at[core], extra_send)

        @pl.when(group > 0)
        def _():
            extra_pass().wait_send()


def solution(mesh):
    rows, groups = mesh.shape["rows"], mesh.shape["lags"]

    def shards(history, incident, kernel, near_blocks, self_inverse):
        lags, waves, block = history.shape
        steps = incident.shape[0]
        slots = near_blocks.shape[2]
        per_chunk = 2 if lags % 2 == 0 else 1
        chunks = lags // per_chunk
        half = rows // 2
        ahead = steps - 1
        f32, bf16 = jnp.float32, jnp.bfloat16
        dma = pltpu.SemaphoreType.DMA
        anywhere = pl.BlockSpec(memory_space=pl.ANY)
        return pl.pallas_call(
            functools.partial(march, rows, groups, per_chunk),
            out_shape=jax.ShapeDtypeStruct((steps, waves, block), f32),
            in_specs=[pl.BlockSpec(memory_space=pltpu.SMEM)] + [anywhere] * 4,
            out_specs=anywhere,
            scratch_shapes=[
                pltpu.VMEM((lags, slots, block, block), f32),
                pltpu.VMEM((lags, slots * block, block), bf16),
                pltpu.VMEM((lags, slots * block, block), bf16),
                pltpu.VMEM((2, half, max(ahead, 1), waves, block), f32),
                pltpu.VMEM((steps, waves, block), f32),
                pltpu.VMEM((groups, steps, waves, block), f32),
                pltpu.VMEM((steps, rows, waves, block), f32),
                pltpu.VMEM((steps, waves, block), f32),
                pltpu.VMEM((block, block), f32),
                pltpu.VMEM((block, block), bf16),
                pltpu.VMEM((block, block), bf16),
                dma((lags,)), dma((2,)), dma((chunks,)), dma((steps,)),
                dma((chunks,)), dma((chunks,)), dma((chunks,)), dma((chunks,)),
                dma, dma, dma, dma, dma((chunks,)), dma((chunks,)),
                dma((steps,)), dma((steps,)), dma((steps,)), dma((steps,)), dma((steps,)), dma((steps,)),
            ]
            + [pltpu.VMEM((2, half, per_chunk, waves, block), f32)] * chunks,
            compiler_params=pltpu.CompilerParams(
                collective_id=0, has_side_effects=True, vmem_limit_bytes=VMEM_LIMIT
            ),
            cost_estimate=pl.CostEstimate(
                flops=6 * steps * lags * slots * waves * block * block,
                bytes_accessed=4 * lags * slots * block * block,
                transcendentals=0,
            ),
        )(jnp.transpose(near_blocks, (2, 0, 1)), history, incident, kernel, self_inverse)

    in_specs = (
        P("lags", None, "rows"),
        P(None, None, "rows"),
        P("rows", "lags", None, None, None),
        P("rows", "lags", None),
        P("rows", None, None),
    )
    return jax.shard_map(
        shards, mesh=mesh, in_specs=in_specs, out_specs=P(None, None, "rows"), check_vma=False
    )
```
